32 devices in a mesh: row: 4 (over x, core), col: 8 (over z, y).
Axes of the slice: x: 2, y: 2, z: 4, core: 2. Of those that a mesh axis runs over, the one named last changes fastest.
Arguments:
- pair: bfloat16 [128, 128, 128], P('row', 'col'), may hold values from -6 to 6
- conv_weight: bfloat16 [3, 3, 128, 128], replicated, may hold values from -0.1875 to 0.1875
- conv_bias: float32 [128], replicated, may hold values from -3 to 3
- norm_gain: float32 [128], replicated, may hold values from 0.1 to 1.9
- norm_shift: float32 [128], replicated, may hold values from -2.5 to 2.5
- proj_weight: bfloat16 [128, 512], replicated, may hold values from -0.5 to 0.5
- gate_weight: bfloat16 [128, 128], replicated, may hold values from -0.5 to 0.5
- tri_gain: float32 [128], replicated, may hold values from 0.1 to 1.9
- tri_shift: float32 [128], replicated, may hold values from -2.5 to 2.5
- out_weight: bfloat16 [128, 128], replicated, may hold values from -0.5 to 0.5
Outputs:
- updated: bfloat16 [128, 128, 128], P('row', 'col')
The draws below stay inside these ranges and needn't reach their ends.
All inputs are finite; a program needn't handle non-finite values.
Results may differ from the reference program's by a relative error of at most 0.0051.
Values may be sent and summed in bfloat16 or wider, within the bound.
A program may use at most 64 MiB of HBM per device.

```python
import jax
import jax.numpy as jnp
from jax import lax

C = 128
CH = 128
DILATION_STEP = 2
CROP = 128


def block_levels(rng, extent, shards, least, largest):
    factor_of = 1.0
    for dim, shards_of in shards:
        heights = jax.random.uniform(jax.random.fold_in(jax.random.fold_in(rng, 6), dim), (shards_of,), jnp.float32, least / len(shards), largest / len(shards))
        factor_of = factor_of * jnp.repeat(jnp.exp(heights), extent[dim] // shards_of).reshape((-1,) + (1,) * (len(extent) - 1 - dim))
    return factor_of


def normal_values(stream_key, extent, scale, limit, pieces=(), held_as=jnp.bfloat16):
    values = scale * jax.random.normal(stream_key, extent, jnp.float32)
    if pieces:
        values = values * block_levels(stream_key, extent, pieces, -0.22, 0.18)
    return jnp.clip(values, -limit, limit).astype(held_as)


def setup_inputs(seed: int = 0) -> dict:
    key_of = jax.random.split(jax.random.key(seed), 11)
    pair = normal_values(key_of[0], (CROP, CROP, C), 1.0, 6.0, ((0, 4), (1, 8)))
    conv_weight = normal_values(key_of[1], (3, 3, C, C), (9 * C) ** -0.5, 0.1875)
    conv_bias = normal_values(key_of[2], (C,), 0.5, 3.0, (), jnp.float32)
    norm_gain = jnp.clip(1.0 + 0.18 * jax.random.normal(key_of[3], (C,), jnp.float32), 0.1, 1.9)
    norm_shift = normal_values(key_of[4], (C,), 0.4, 2.5, (), jnp.float32)
    proj_weight = normal_values(key_of[5], (C, 4 * CH), C ** -0.5, 0.5)
    gate_weight = normal_values(key_of[6], (C, C), C ** -0.5, 0.5)
    tri_gain = jnp.clip(1.0 + 0.18 * jax.random.normal(key_of[7], (CH,), jnp.float32), 0.1, 1.9)
    tri_shift = normal_values(key_of[8], (CH,), 0.4, 2.5, (), jnp.float32)
    out_weight = normal_values(key_of[9], (CH, C), CH ** -0.5, 0.5)
    return {"pair": pair, "conv_weight": conv_weight, "conv_bias": conv_bias, "norm_gain": norm_gain, "norm_shift": norm_shift, "proj_weight": proj_weight, "gate_weight": gate_weight, "tri_gain": tri_gain, "tri_shift": tri_shift, "out_weight": out_weight}


def layer_norm(values, gain, shift):
    row_mean = lax.optimization_barrier(jnp.mean(values, -1, keepdims=True))
    centred = values - row_mean
    variance = lax.optimization_barrier(jnp.mean(centred * centred, -1, keepdims=True))
    return centred * lax.rsqrt(variance + 1e-05) * gain + shift

def reference(pair, conv_weight, conv_bias, norm_gain, norm_shift, proj_weight, gate_weight, tri_gain, tri_shift, out_weight):
    pair_length = pair.shape[0]
    channels = pair.shape[2]
    padded_pair = jnp.pad(pair, ((DILATION_STEP, DILATION_STEP), (DILATION_STEP, DILATION_STEP), (0, 0)))
    total = pair.astype(jnp.float32) + conv_bias
    for kernel_row in range(3):
        for kernel_column in range(3):
            kernel_window = padded_pair[kernel_row * DILATION_STEP:kernel_row * DILATION_STEP + pair_length, kernel_column * DILATION_STEP:kernel_column * DILATION_STEP + pair_length, :]
            product = jnp.dot(kernel_window.reshape(pair_length * pair_length, channels), conv_weight[kernel_row, kernel_column], preferred_element_type=jnp.float32)
            total = total + product.reshape(pair_length, pair_length, channels)
    hidden = lax.optimization_barrier(total.astype(jnp.bfloat16))
    normed = layer_norm(hidden.astype(jnp.float32), norm_gain, norm_shift).astype(jnp.bfloat16)
    flat = normed.reshape(pair_length * pair_length, channels)
    proj = jnp.dot(flat, proj_weight, preferred_element_type=jnp.float32)
    left = (jax.nn.sigmoid(proj[:, :CH]) * proj[:, CH:2 * CH]).astype(jnp.bfloat16).reshape(pair_length, pair_length, CH)
    right = (jax.nn.sigmoid(proj[:, 2 * CH:3 * CH]) * proj[:, 3 * CH:]).astype(jnp.bfloat16).reshape(pair_length, pair_length, CH)
    gate = jax.nn.sigmoid(jnp.dot(flat, gate_weight, preferred_element_type=jnp.float32))
    tri = jnp.einsum('ikc,jkc->ijc', left.astype(jnp.float32), right.astype(jnp.float32))
    tnorm = layer_norm(tri, tri_gain, tri_shift).astype(jnp.bfloat16).reshape(pair_length * pair_length, CH)
    update = jnp.dot(tnorm, out_weight, preferred_element_type=jnp.float32)
    result = hidden.astype(jnp.float32).reshape(pair_length * pair_length, channels) + gate * update
    return result.astype(jnp.bfloat16).reshape(pair_length, pair_length, channels)
```

```python
import functools

import jax
import jax.numpy as jnp
from jax import lax
from jax.experimental import pallas as pl
from jax.experimental.pallas import tpu as pltpu
from jax.sharding import PartitionSpec as P

STEP = 2
EDGE = 8
SIDES = ((-1, 0), (1, 0), (0, -1), (0, 1), (-1, -1), (-1, 1), (1, -1), (1, 1))
F32, BF16 = jnp.float32, jnp.bfloat16


def layer_norm(values, gain, shift):
    row_mean = jnp.mean(values, -1, keepdims=True)
    centred = values - row_mean
    variance = jnp.mean(centred * centred, -1, keepdims=True)
    return centred * lax.rsqrt(variance + 1e-05) * gain + shift


def swap_blocks(parts, width):
    count = len(parts)
    parts = list(parts)
    lane = lax.broadcasted_iota(jnp.int32, parts[0].shape, 1)
    bit = 1
    while bit < count:
        low = (lane & (bit * width)) == 0
        for p in range(count):
            if p & bit == 0:
                a, b = parts[p], parts[p + bit]
                parts[p] = jnp.where(low, a, pltpu.roll(b, bit * width, 1))
                parts[p + bit] = jnp.where(low, pltpu.roll(a, 128 - bit * width, 1), b)
        bit *= 2
    return parts


def kernel(
    sizes,
    pair, conv_w, conv_b, n_gain, n_shift, proj_w, gate_w, t_gain, t_shift, out_w,
    out,
    padded, strips, halo_row, halo_col, halo_cor, hidden, gate,
    send_l, send_r, all_l, all_r, left32, acc, send_t, all_t, update,
    halo_s, halo_r, l_s, l_r, r_s, r_r, g_s, g_r, t_s, t_r,
):
    n_row, n, rows, cols = sizes
    group = rows // n
    width = 128 // n
    flat = rows * cols
    half = rows // 2
    r, c = lax.axis_index("row"), lax.axis_index("col")

    def exists(dr, dc):
        ok = None
        if dr:
            ok = (r + dr >= 0) & (r + dr < n_row)
        if dc:
            col_ok = (c + dc >= 0) & (c + dc < n)
            ok = col_ok if ok is None else ok & col_ok
        return ok

    barrier = pltpu.get_barrier_semaphore()
    for k in range(1, n):
        pl.semaphore_signal(barrier, inc=1, device_id=(r, lax.rem(c + k, n)), device_id_type=pl.DeviceIdType.MESH)
    for k in range(1, n_row):
        pl.semaphore_signal(barrier, inc=1, device_id=(lax.rem(r + k, n_row), c), device_id_type=pl.DeviceIdType.MESH)
    for dr, dc in SIDES[4:]:
        @pl.when(exists(dr, dc))
        def _():
            pl.semaphore_signal(barrier, inc=1, device_id=(r + dr, c + dc), device_id_type=pl.DeviceIdType.MESH)

    padded[...] = jnp.zeros_like(padded)
    padded[STEP : STEP + rows, EDGE : EDGE + cols, :] = pair[...].astype(F32)
    for at, col in enumerate((0, 1, cols - 2, cols - 1)):
        strips[at] = padded[STEP : STEP + rows, EDGE + col, :].astype(BF16)

    beside_r = (r > 0).astype(jnp.int32) + (r < n_row - 1).astype(jnp.int32)
    beside_c = (c > 0).astype(jnp.int32) + (c < n - 1).astype(jnp.int32)
    pl.semaphore_wait(barrier, n - 1 + n_row - 1 + beside_r * beside_c)

    def halo_copy(at, dr, dc):
        if dc == 0:
            src = pair.at[pl.ds(0 if dr < 0 else rows - STEP, STEP)]
            dst = halo_row.at[1 if dr < 0 else 0]
        else:
            src = strips.at[pl.ds(0 if dc < 0 else 2, 2)]
            if dr == 0:
                dst = halo_col.at[1 if dc < 0 else 0]
            else:
                src = strips.at[pl.ds(0 if dc < 0 else 2, 2), pl.ds(0 if dr < 0 else rows - 16, 16)]
                dst = halo_cor.at[at - 4]
        return pltpu.make_async_remote_copy(
            src_ref=src, dst_ref=dst, send_sem=halo_s.at[at], recv_sem=halo_r.at[at],
            device_id=(r + dr, c + dc), device_id_type=pl.DeviceIdType.MESH,
        )

    for at, (dr, dc) in enumerate(SIDES):
        @pl.when(exists(dr, dc))
        def _():
            halo_copy(at, dr, dc).start()

    for at, (dr, dc) in enumerate(SIDES):
        @pl.when(exists(-dr, -dc))
        def _():
            halo_copy(at, dr, dc).wait_recv()
            first_row = 0 if dr > 0 else STEP + rows
            first_col = EDGE - 2 if dc > 0 else EDGE + cols
            if dc == 0:
                padded[first_row : first_row + STEP, EDGE : EDGE + cols, :] = halo_row[1 if dr < 0 else 0].astype(F32)
            elif dr == 0:
                got = halo_col[1 if dc < 0 else 0].astype(F32)
                for j in range(2):
                    padded[STEP : STEP + rows, first_col + j, :] = got[j]
            else:
                got = halo_cor[at - 4].astype(F32)
                part = slice(0, 2) if dr < 0 else slice(14, 16)
                for j in range(2):
                    padded[first_row : first_row + STEP, first_col + j, :] = got[j, part]

    shifted = [
        padded[:, EDGE + STEP * b : EDGE + STEP * b + cols, :].astype(BF16) for b in (-1, 0, 1)
    ]
    wide = jnp.concatenate(shifted, axis=2)
    total = pair[...].astype(F32).reshape(flat, 128) + conv_b[...]
    for a in range(3):
        total = total + jnp.dot(
            wide[a * STEP : a * STEP + rows].reshape(flat, 3 * 128), conv_w[a],
            preferred_element_type=F32,
        )
    rounded = total.astype(BF16)
    hidden[...] = rounded
    normed = layer_norm(rounded.astype(F32), n_gain[...], n_shift[...]).astype(BF16)

    def gated(first):
        part = jnp.dot(normed, proj_w[:, first : first + 256], preferred_element_type=F32)
        return jax.nn.sigmoid(part[:, :128]) * part[:, 128:]

    step = group * cols

    def scatter(values, sent, whole):
        packed = swap_blocks([values[p * step : (p + 1) * step] for p in range(n)], width)
        for p in range(n):
            sent[p] = packed[p].astype(BF16).reshape(group, cols, 128)

    def block_copy(k, sent, whole, s_sem, r_sem):
        to = lax.rem(c + k, n)
        return pltpu.make_async_remote_copy(
            src_ref=sent.at[to], dst_ref=whole.at[c], send_sem=s_sem.at[k], recv_sem=r_sem.at[k],
            device_id=(r, to), device_id_type=pl.DeviceIdType.MESH,
        )

    mine_r = all_r.at[r]
    scatter(gated(256), send_r, mine_r)
    for k in range(1, n):
        block_copy(k, send_r, mine_r, r_s, r_r).start()
    scatter(gated(0), send_l, all_l)
    for k in range(1, n):
        block_copy(k, send_l, all_l, l_s, l_r).start()
    all_r[r, c] = send_r[c]
    all_l[c] = send_l[c]
    gate[...] = jax.nn.sigmoid(jnp.dot(normed, gate_w[...], preferred_element_type=F32))

    for k in range(1, n):
        block_copy(k, send_r, mine_r, r_s, r_r).wait_recv()

    def row_copy(k):
        to = lax.rem(r + k, n_row)
        return pltpu.make_async_remote_copy(
            src_ref=all_r.at[r], dst_ref=all_r.at[r], send_sem=g_s.at[k], recv_sem=g_r.at[k],
            device_id=(to, c), device_id_type=pl.DeviceIdType.MESH,
        )

    for k in range(1, n_row):
        row_copy(k).start()
    for k in range(1, n):
        block_copy(k, send_l, all_l, l_s, l_r).wait_recv()
    for g in range(group):
        left32[g] = all_l[:, g].reshape(n * cols, 128).astype(F32)

    lane_block = lax.broadcasted_iota(jnp.int32, (half, 128), 1) // width
    turn = lax.broadcasted_iota(jnp.int32, (half, 128), 0) // group
    first_half = ((lane_block - turn + n) & (n - 1)) < n // 2

    def back_copy(to, at):
        return pltpu.make_async_remote_copy(
            src_ref=send_t.at[to], dst_ref=all_t.at[c], send_sem=t_s.at[to], recv_sem=t_r.at[at],
            device_id=(r, to), device_id_type=pl.DeviceIdType.MESH,
        )

    def one_row_block(s, _):
        rp = lax.rem(r - s + n_row, n_row)

        @pl.when(s > 0)
        def _():
            pltpu.make_async_remote_copy(
                src_ref=all_r.at[rp], dst_ref=all_r.at[rp], send_sem=g_s.at[s], recv_sem=g_r.at[s],
                device_id=(rp, c), device_id_type=pl.DeviceIdType.MESH,
            ).wait_recv()

        def one_group(gj, _):
            right = all_r[rp, :, gj].reshape(n * cols, 128).astype(F32)
            for rho in range(n):
                turned = pltpu.roll(right, rho * width, 1) if rho else right
                for gi in range(group):
                    acc[gi, pl.ds(rho * group + gj, 1), :] = jnp.sum(
                        left32[gi] * turned, axis=0, keepdims=True
                    )
            return 0

        lax.fori_loop(0, group, one_group, 0)
        for gi in range(group):
            low, high = acc[gi, :half], acc[gi, half:]
            send_t[2 * rp, gi] = jnp.where(first_half, low, high).astype(BF16)
            send_t[2 * rp + 1, gi] = jnp.where(first_half, high, low).astype(BF16)
        for h in range(2):
            to = 2 * rp + h

            @pl.when(to != c)
            def _():
                back_copy(to, c).start()

            @pl.when(to == c)
            def _():
                all_t[c] = send_t[c]

        return 0

    lax.fori_loop(0, n_row, one_row_block, 0)

    for k in range(1, n):
        at = lax.rem(c + k, n)
        back_copy(at, at).wait_recv()
    parts = swap_blocks([all_t[p].astype(F32).reshape(group * half, 128) for p in range(n)], width)
    tri = jnp.concatenate(parts, axis=0)
    tnorm = layer_norm(tri, t_gain[...], t_shift[...]).astype(BF16)
    moved = jnp.dot(tnorm, out_w[...], preferred_element_type=F32)
    for b in range(n):
        for gi in range(group):
            for rho in range(n // 2):
                at = (b * group + gi) * half + rho * group
                j = ((b - rho) % (n // 2)) * group
                update[b * group + gi, j : j + group, :] = moved[at : at + group]
    result = hidden[...].astype(F32) + gate[...] * update[...].reshape(flat, 128)
    out[...] = result.astype(BF16).reshape(rows, cols, 128)

    for at, (dr, dc) in enumerate(SIDES):
        @pl.when(exists(dr, dc))
        def _():
            halo_copy(at, dr, dc).wait_send()
    for k in range(1, n):
        block_copy(k, send_r, mine_r, r_s, r_r).wait_send()
        block_copy(k, send_l, all_l, l_s, l_r).wait_send()
        back_copy(lax.rem(c + k, n), c).wait_send()
    for k in range(1, n_row):
        row_copy(k).wait_send()


def on_device(n_row, n, pair, conv_weight, conv_bias, norm_gain, norm_shift, proj_weight,
              gate_weight, tri_gain, tri_shift, out_weight):
    rows, cols, channels = pair.shape
    group = rows // n
    flat = rows * cols
    dma = pltpu.SemaphoreType.DMA
    flat_vec = lambda v: v.reshape(1, 128)
    return pl.pallas_call(
        functools.partial(kernel, (n_row, n, rows, cols)),
        out_shape=jax.ShapeDtypeStruct(pair.shape, BF16),
        in_specs=[pl.BlockSpec(memory_space=pltpu.VMEM)] * 10,
        out_specs=pl.BlockSpec(memory_space=pltpu.VMEM),
        scratch_shapes=[
            pltpu.VMEM((rows + 2 * STEP, EDGE + cols + 8, 128), F32),
            pltpu.VMEM((4, rows, 128), BF16),
            pltpu.VMEM((2, STEP, cols, 128), BF16),
            pltpu.VMEM((2, 2, rows, 128), BF16),
            pltpu.VMEM((4, 2, 16, 128), BF16),
            pltpu.VMEM((flat, 128), BF16),
            pltpu.VMEM((flat, 128), F32),
            pltpu.VMEM((n, group, cols, 128), BF16),
            pltpu.VMEM((n, group, cols, 128), BF16),
            pltpu.VMEM((n, group, cols, 128), BF16),
            pltpu.VMEM((n_row, n, group, cols, 128), BF16),
            pltpu.VMEM((group, n * cols, 128), F32),
            pltpu.VMEM((group, rows, 128), F32),
            pltpu.VMEM((n, group, rows // 2, 128), BF16),
            pltpu.VMEM((n, group, rows // 2, 128), BF16),
            pltpu.VMEM((rows, cols, 128), F32),
            dma((8,)), dma((8,)), dma((n,)), dma((n,)), dma((n,)), dma((n,)),
            dma((n_row,)), dma((n_row,)), dma((n,)), dma((n,)),
        ],
        compiler_params=pltpu.CompilerParams(
            collective_id=0, has_side_effects=True, vmem_limit_bytes=48 * 1024 * 1024
        ),
    )(
        pair, conv_weight.reshape(3, 3 * 128, 128), flat_vec(conv_bias), flat_vec(norm_gain),
        flat_vec(norm_shift), proj_weight, gate_weight, flat_vec(tri_gain), flat_vec(tri_shift),
        out_weight,
    )


def solution(mesh):
    placed = (P("row", "col", None),) + (P(),) * 9
    return jax.shard_map(
        functools.partial(on_device, mesh.shape["row"], mesh.shape["col"]),
        mesh=mesh, in_specs=placed, out_specs=P("row", "col", None), check_vma=False,
    )
```

```python
import functools

import jax
import jax.numpy as jnp
from jax import lax
from jax.experimental import pallas as pl
from jax.experimental.pallas import tpu as pltpu
from jax.sharding import PartitionSpec as P

STEP = 2
EDGE = 8
SIDES = ((-1, 0), (1, 0), (0, -1), (0, 1), (-1, -1), (-1, 1), (1, -1), (1, 1))
F32, BF16 = jnp.float32, jnp.bfloat16


def layer_norm(values, gain, shift):
    row_mean = jnp.mean(values, -1, keepdims=True)
    centred = values - row_mean
    variance = jnp.mean(centred * centred, -1, keepdims=True)
    return centred * lax.rsqrt(variance + 1e-05) * gain + shift


def swap_blocks(parts, width):
    count = len(parts)
    parts = list(parts)
    lane = lax.broadcasted_iota(jnp.int32, parts[0].shape, 1)
    bit = 1
    while bit < count:
        low = (lane & (bit * width)) == 0
        for p in range(count):
            if p & bit == 0:
                a, b = parts[p], parts[p + bit]
                parts[p] = jnp.where(low, a, pltpu.roll(b, bit * width, 1))
                parts[p + bit] = jnp.where(low, pltpu.roll(a, 128 - bit * width, 1), b)
        bit *= 2
    return parts


def kernel(
    sizes,
    pair_in, conv_w_in, conv_b_in, n_gain_in, n_shift_in, proj_w_in, gate_w_in, t_gain_in, t_shift_in, out_w_in,
    out,
    pair, conv_w, conv_b, n_gain, n_shift, proj_w, gate_w, t_gain, t_shift, out_w,
    padded, strips, halo_row, halo_col, halo_cor, hidden, gate,
    send_l, send_r, all_l, all_r, left32, acc, send_t, all_t, update,
    in_s, halo_s, halo_r, l_s, l_r, r_s, r_r, x_s, x_r, g_s, g_r, t_s, t_r,
):
    n_row, n, rows, cols = sizes
    group = rows // n
    width = 128 // n
    flat = rows * cols
    half = rows // 2
    r, c = lax.axis_index("row"), lax.axis_index("col")

    loads = [
        pltpu.make_async_copy(src, dst, in_s.at[at])
        for at, (src, dst) in enumerate((
            (pair_in, pair), (conv_w_in, conv_w), (conv_b_in, conv_b), (n_gain_in, n_gain),
            (n_shift_in, n_shift), (proj_w_in, proj_w), (gate_w_in, gate_w), (t_gain_in, t_gain),
            (t_shift_in, t_shift), (out_w_in, out_w),
        ))
    ]
    for load in loads:
        load.start()

    def exists(dr, dc):
        ok = None
        if dr:
            ok = (r + dr >= 0) & (r + dr < n_row)
        if dc:
            col_ok = (c + dc >= 0) & (c + dc < n)
            ok = col_ok if ok is None else ok & col_ok
        return ok

    barrier = pltpu.get_barrier_semaphore()
    for k in range(1, n):
        pl.semaphore_signal(barrier, inc=1, device_id=(r, lax.rem(c + k, n)), device_id_type=pl.DeviceIdType.MESH)
    for k in range(1, n_row):
        pl.semaphore_signal(barrier, inc=1, device_id=(lax.rem(r + k, n_row), c), device_id_type=pl.DeviceIdType.MESH)
    for dr, dc in SIDES[4:]:
        @pl.when(exists(dr, dc))
        def _():
            pl.semaphore_signal(barrier, inc=1, device_id=(r + dr, c + dc), device_id_type=pl.DeviceIdType.MESH)

    padded[...] = jnp.zeros_like(padded)
    loads[0].wait()
    padded[STEP : STEP + rows, EDGE : EDGE + cols, :] = pair[...].astype(F32)
    for at, col in enumerate((0, 1, cols - 2, cols - 1)):
        strips[at] = padded[STEP : STEP + rows, EDGE + col, :].astype(BF16)

    beside_r = (r > 0).astype(jnp.int32) + (r < n_row - 1).astype(jnp.int32)
    beside_c = (c > 0).astype(jnp.int32) + (c < n - 1).astype(jnp.int32)
    pl.semaphore_wait(barrier, n - 1 + n_row - 1 + beside_r * beside_c)

    def halo_copy(at, dr, dc):
        if dc == 0:
            src = pair.at[pl.ds(0 if dr < 0 else rows - STEP, STEP)]
            dst = halo_row.at[1 if dr < 0 else 0]
        else:
            src = strips.at[pl.ds(0 if dc < 0 else 2, 2)]
            if dr == 0:
                dst = halo_col.at[1 if dc < 0 else 0]
            else:
                src = strips.at[pl.ds(0 if dc < 0 else 2, 2), pl.ds(0 if dr < 0 else rows - 16, 16)]
                dst = halo_cor.at[at - 4]
        return pltpu.make_async_remote_copy(
            src_ref=src, dst_ref=dst, send_sem=halo_s.at[at], recv_sem=halo_r.at[at],
            device_id=(r + dr, c + dc), device_id_type=pl.DeviceIdType.MESH,
        )

    for at, (dr, dc) in enumerate(SIDES):
        @pl.when(exists(dr, dc))
        def _():
            halo_copy(at, dr, dc).start()

    for load in loads[1:]:
        load.wait()
    for at, (dr, dc) in enumerate(SIDES):
        @pl.when(exists(-dr, -dc))
        def _():
            halo_copy(at, dr, dc).wait_recv()
            first_row = 0 if dr > 0 else STEP + rows
            first_col = EDGE - 2 if dc > 0 else EDGE + cols
            if dc == 0:
                padded[first_row : first_row + STEP, EDGE : EDGE + cols, :] = halo_row[1 if dr < 0 else 0].astype(F32)
            elif dr == 0:
                got = halo_col[1 if dc < 0 else 0].astype(F32)
                for j in range(2):
                    padded[STEP : STEP + rows, first_col + j, :] = got[j]
            else:
                got = halo_cor[at - 4].astype(F32)
                part = slice(0, 2) if dr < 0 else slice(14, 16)
                for j in range(2):
                    padded[first_row : first_row + STEP, first_col + j, :] = got[j, part]

    shifted = [
        padded[:, EDGE + STEP * b : EDGE + STEP * b + cols, :].astype(BF16) for b in (-1, 0, 1)
    ]
    wide = jnp.concatenate(shifted, axis=2)
    total = pair[...].astype(F32).reshape(flat, 128) + conv_b[...]
    for a in range(3):
        total = total + jnp.dot(
            wide[a * STEP : a * STEP + rows].reshape(flat, 3 * 128), conv_w[a],
            preferred_element_type=F32,
        )
    rounded = total.astype(BF16)
    hidden[...] = rounded
    normed = layer_norm(rounded.astype(F32), n_gain[...], n_shift[...]).astype(BF16)

    def gated(first):
        part = jnp.dot(normed, proj_w[:, first : first + 256], preferred_element_type=F32)
        return jax.nn.sigmoid(part[:, :128]) * part[:, 128:]

    step = group * cols

    def scatter(values, sent):
        packed = swap_blocks([values[p * step : (p + 1) * step] for p in range(n)], width)
        for p in range(n):
            sent[p] = packed[p].astype(BF16).reshape(group, cols, 128)

    def block_copy(k, sent, whole, s_sem, r_sem):
        to = lax.rem(c + k, n)
        return pltpu.make_async_remote_copy(
            src_ref=sent.at[to], dst_ref=whole.at[c], send_sem=s_sem.at[k], recv_sem=r_sem.at[k],
            device_id=(r, to), device_id_type=pl.DeviceIdType.MESH,
        )

    n_chip = n_row // 2
    chip, core = r // 2, lax.rem(r, 2)
    beside = chip * 2 + 1 - core

    def row_of(s):
        return lax.rem(chip - s // 2 + n_chip, n_chip) * 2 + lax.rem(core + s, 2)

    def chip_copy(m, at):
        return pltpu.make_async_remote_copy(
            src_ref=all_r.at[r, at], dst_ref=all_r.at[r, at],
            send_sem=x_s.at[m, at], recv_sem=x_r.at[m, at],
            device_id=(lax.rem(chip + m, n_chip) * 2 + core, c), device_id_type=pl.DeviceIdType.MESH,
        )

    def core_copy(s):
        row = row_of(s)
        return pltpu.make_async_remote_copy(
            src_ref=all_r.at[row], dst_ref=all_r.at[row],
            send_sem=g_s.at[s], recv_sem=g_r.at[s],
            device_id=(beside, c), device_id_type=pl.DeviceIdType.MESH,
        )

    mine_r = all_r.at[r]
    scatter(gated(256), send_r)
    for k in range(1, n):
        block_copy(k, send_r, mine_r, r_s, r_r).start()
    all_r[r, c] = send_r[c]
    for m in range(1, n_chip):
        chip_copy(m, c).start()
    scatter(gated(0), send_l)
    for k in range(1, n):
        block_copy(k, send_l, all_l, l_s, l_r).start()
    all_l[c] = send_l[c]
    for k in range(1, n):
        block_copy(k, send_r, mine_r, r_s, r_r).wait_recv()
        for m in range(1, n_chip):
            chip_copy(m, lax.rem(c + n - k, n)).start()
    core_copy(0).start()
    gate[...] = jax.nn.sigmoid(jnp.dot(normed, gate_w[...], preferred_element_type=F32))
    for k in range(1, n):
        block_copy(k, send_l, all_l, l_s, l_r).wait_recv()
    for g in range(group):
        left32[g] = all_l[:, g].reshape(n * cols, 128).astype(F32)

    lane_block = lax.broadcasted_iota(jnp.int32, (half, 128), 1) // width
    turn = lax.broadcasted_iota(jnp.int32, (half, 128), 0) // group
    first_half = ((lane_block - turn + n) & (n - 1)) < n // 2

    def back_copy(to, at):
        return pltpu.make_async_remote_copy(
            src_ref=send_t.at[to], dst_ref=all_t.at[c], send_sem=t_s.at[to], recv_sem=t_r.at[at],
            device_id=(r, to), device_id_type=pl.DeviceIdType.MESH,
        )

    def one_row_block(s, _):
        rp = row_of(s)
        even = lax.rem(s, 2) == 0

        @pl.when(even & (s > 0))
        def _():
            for at in range(n):
                pltpu.make_async_remote_copy(
                    src_ref=all_r.at[rp, at], dst_ref=all_r.at[rp, at],
                    send_sem=x_s.at[s // 2, at], recv_sem=x_r.at[s // 2, at],
                    device_id=(rp, c), device_id_type=pl.DeviceIdType.MESH,
                ).wait_recv()
            core_copy(s).start()

        @pl.when(jnp.logical_not(even))
        def _():
            pltpu.make_async_remote_copy(
                src_ref=all_r.at[rp], dst_ref=all_r.at[rp],
                send_sem=g_s.at[s - 1], recv_sem=g_r.at[s - 1],
                device_id=(beside, c), device_id_type=pl.DeviceIdType.MESH,
            ).wait_recv()

        def one_group(gj, _):
            right = all_r[rp, :, gj].reshape(n * cols, 128).astype(F32)
            for rho in range(n):
                turned = pltpu.roll(right, rho * width, 1) if rho else right
                for gi in range(group):
                    acc[gi, pl.ds(rho * group + gj, 1), :] = jnp.sum(
                        left32[gi] * turned, axis=0, keepdims=True
                    )
            return 0

        lax.fori_loop(0, group, one_group, 0)
        for gi in range(group):
            low, high = acc[gi, :half], acc[gi, half:]
            send_t[2 * rp, gi] = jnp.where(first_half, low, high).astype(BF16)
            send_t[2 * rp + 1, gi] = jnp.where(first_half, high, low).astype(BF16)
        for h in range(2):
            to = 2 * rp + h

            @pl.when(to != c)
            def _():
                back_copy(to, c).start()

            @pl.when(to == c)
            def _():
                all_t[c] = send_t[c]

        return 0

    lax.fori_loop(0, n_row, one_row_block, 0)

    for k in range(1, n):
        at = lax.rem(c + k, n)
        back_copy(at, at).wait_recv()
    parts = swap_blocks([all_t[p].astype(F32).reshape(group * half, 128) for p in range(n)], width)
    tri = jnp.concatenate(parts, axis=0)
    tnorm = layer_norm(tri, t_gain[...], t_shift[...]).astype(BF16)
    moved = jnp.dot(tnorm, out_w[...], preferred_element_type=F32)
    for b in range(n):
        for gi in range(group):
            for rho in range(n // 2):
                at = (b * group + gi) * half + rho * group
                j = ((b - rho) % (n // 2)) * group
                update[b * group + gi, j : j + group, :] = moved[at : at + group]
    result = hidden[...].astype(F32) + gate[...] * update[...].reshape(flat, 128)
    out[...] = result.astype(BF16).reshape(rows, cols, 128)

    for at, (dr, dc) in enumerate(SIDES):
        @pl.when(exists(dr, dc))
        def _():
            halo_copy(at, dr, dc).wait_send()
    for k in range(1, n):
        block_copy(k, send_r, mine_r, r_s, r_r).wait_send()
        block_copy(k, send_l, all_l, l_s, l_r).wait_send()
        back_copy(lax.rem(c + k, n), c).wait_send()
    for m in range(n_chip):
        core_copy(2 * m).wait_send()
        for at in range(n):
            if m:
                chip_copy(m, at).wait_send()


def on_device(n_row, n, pair, conv_weight, conv_bias, norm_gain, norm_shift, proj_weight,
              gate_weight, tri_gain, tri_shift, out_weight):
    rows, cols, channels = pair.shape
    group = rows // n
    flat = rows * cols
    dma = pltpu.SemaphoreType.DMA
    flat_vec = lambda v: v.reshape(1, 128)
    return pl.pallas_call(
        functools.partial(kernel, (n_row, n, rows, cols)),
        out_shape=jax.ShapeDtypeStruct(pair.shape, BF16),
        in_specs=[pl.BlockSpec(memory_space=pltpu.HBM)] * 10,
        out_specs=pl.BlockSpec(memory_space=pltpu.VMEM),
        scratch_shapes=[
            pltpu.VMEM((rows, cols, 128), BF16),
            pltpu.VMEM((3, 3 * 128, 128), BF16),
            *[pltpu.VMEM((1, 128), F32)] * 3,
            pltpu.VMEM((128, 512), BF16),
            pltpu.VMEM((128, 128), BF16),
            *[pltpu.VMEM((1, 128), F32)] * 2,
            pltpu.VMEM((128, 128), BF16),
            pltpu.VMEM((rows + 2 * STEP, EDGE + cols + 8, 128), F32),
            pltpu.VMEM((4, rows, 128), BF16),
            pltpu.VMEM((2, STEP, cols, 128), BF16),
            pltpu.VMEM((2, 2, rows, 128), BF16),
            pltpu.VMEM((4, 2, 16, 128), BF16),
            pltpu.VMEM((flat, 128), BF16),
            pltpu.VMEM((flat, 128), F32),
            pltpu.VMEM((n, group, cols, 128), BF16),
            pltpu.VMEM((n, group, cols, 128), BF16),
            pltpu.VMEM((n, group, cols, 128), BF16),
            pltpu.VMEM((n_row, n, group, cols, 128), BF16),
            pltpu.VMEM((group, n * cols, 128), F32),
            pltpu.VMEM((group, rows, 128), F32),
            pltpu.VMEM((n, group, rows // 2, 128), BF16),
            pltpu.VMEM((n, group, rows // 2, 128), BF16),
            pltpu.VMEM((rows, cols, 128), F32),
            dma((10,)), dma((8,)), dma((8,)), dma((n,)), dma((n,)), dma((n,)), dma((n,)),
            dma((n_row // 2, n)), dma((n_row // 2, n)),
            dma((n_row,)), dma((n_row,)), dma((n,)), dma((n,)),
        ],
        compiler_params=pltpu.CompilerParams(
            collective_id=0, has_side_effects=True, vmem_limit_bytes=48 * 1024 * 1024
        ),
    )(
        pair, conv_weight.reshape(3, 3 * 128, 128), flat_vec(conv_bias), flat_vec(norm_gain),
        flat_vec(norm_shift), proj_weight, gate_weight, flat_vec(tri_gain), flat_vec(tri_shift),
        out_weight,
    )


def solution(mesh):
    placed = (P("row", "col", None),) + (P(),) * 9
    return jax.shard_map(
        functools.partial(on_device, mesh.shape["row"], mesh.shape["col"]),
        mesh=mesh, in_specs=placed, out_specs=P("row", "col", None), check_vma=False,
    )
```
